128 devices in a mesh: head: 8 (over z, x_lo), ctx: 16 (over y, x_hi, core).
Axes of the slice: x: 4 (x_hi: 2, x_lo: 2; x = x_hi * 2 + x_lo), y: 4, z: 4, core: 2. Of those that a mesh axis runs over, the one named last changes fastest.
Arguments:
- step_inputs: bfloat16 [2, 8, 8192], P(None, None, 'ctx'), may hold values from -8 to 8
- attn_gain: bfloat16 [8192], P('ctx'), may hold values from 0.5 to 1.5
- mlp_gain: bfloat16 [8192], P('ctx'), may hold values from 0.5 to 1.5
- qkv_trainer: bfloat16 [8192, 10240], P(None, ('head', 'ctx')), may hold values from -0.0625 to 0.0625
- o_trainer: bfloat16 [8192, 8192], P(('head', 'ctx')), may hold values from -0.5 to 0.5
- gate_trainer: bfloat16 [8192, 28672], P(None, ('head', 'ctx')), may hold values from -0.0625 to 0.0625
- up_trainer: bfloat16 [8192, 28672], P(None, ('head', 'ctx')), may hold values from -0.0625 to 0.0625
- down_trainer: bfloat16 [28672, 8192], P(('head', 'ctx')), may hold values from -0.03125 to 0.03125
- key_page_pool: bfloat16 [2048, 128, 1024], P('ctx', None, 'head'), may hold values from -140 to 140
- value_page_pool: bfloat16 [2048, 128, 1024], P('ctx', None, 'head'), may hold values from -6 to 6
- page_table: int32 [8, 256], replicated, may hold values from 0 to 127, as said below
- lengths: int32 [8], replicated, may hold values from 1 to 32766
- shard_map: int32 [8, 16], P('head'), may hold values from 0 to 15, as said below
Outputs:
- decoded: bfloat16 [2, 8, 8192], P(None, None, 'ctx')
The draws below stay inside these ranges and needn't reach their ends.
Inputs may be any that keep to these rules, and one draw needn't show every extreme that they name: For each ctx index c, the entries page_table[r, b] with b % 16 == c, over all responses, are a permutation of 0 .. 127. `shard_map`: each row is a permutation of 0 .. 15.
All inputs are finite; a program needn't handle non-finite values.
Results may differ from the reference program's by a relative error of at most 0.024.
Values may be sent and summed in bfloat16 or wider, within the bound.
A program may use at most 128 MiB of HBM per device.

```python
import jax
import jax.numpy as jnp
from jax import lax

D = 8192
QUERY_HEADS = 64
KEY_VALUE_HEADS = 8
HEAD_SIZE = 128
FF = 28672
RESPONSE_BATCH = 8
RESPONSE_LENGTH = 32768
PAGE_TOKENS = 128
STEPS = 2
TP_WAYS = 8
CONTEXT_SPLITS = 16
BLOCKS = 256
SLOTS_PER_SPLIT = 128
QKV_COLS = 10240


def column_scales(low_end, high_end):
    ramp = jnp.arange(D, dtype=jnp.float32) / (D - 1)
    return jnp.exp(jnp.log(low_end) + ramp * (jnp.log(high_end) - jnp.log(low_end)))


def draw_step_inputs(key, part):
    key = jax.random.fold_in(key, 14)
    tensor_shape = (STEPS, RESPONSE_BATCH, D)
    base_values = jnp.clip(jax.random.normal(key, tensor_shape, jnp.float32), -4.0, 4.0)
    values = base_values * column_scales(0.5, 2.0)[None, None, :]
    return values.astype(jnp.bfloat16)


def draw_key_page_pool(key, part):
    key = jax.random.fold_in(key, 11)
    tensor_shape = (CONTEXT_SPLITS * SLOTS_PER_SPLIT, PAGE_TOKENS, KEY_VALUE_HEADS * HEAD_SIZE)
    first_key = jax.random.fold_in(key, 0)
    values = jnp.clip(jax.random.normal(first_key, tensor_shape, jnp.float32), -6.0, 6.0)
    return values.astype(jnp.bfloat16)


def draw_page_table(key, part):
    key = jax.random.fold_in(key, 12)
    perm_keys = jax.random.split(key, CONTEXT_SPLITS)
    permuted = jax.vmap(lambda one_key: jax.random.permutation(one_key, SLOTS_PER_SPLIT))(perm_keys)
    local_blocks = BLOCKS // CONTEXT_SPLITS
    block_ids = jnp.arange(BLOCKS, dtype=jnp.int32)
    resp_ids = jnp.arange(RESPONSE_BATCH, dtype=jnp.int32)
    column = resp_ids[:, None] * local_blocks + block_ids[None, :] // CONTEXT_SPLITS
    owner_ids = jnp.broadcast_to(block_ids[None, :] % CONTEXT_SPLITS, (RESPONSE_BATCH, BLOCKS))
    return permuted[owner_ids, column].astype(jnp.int32)


def draw_shard_map(key, part):
    key = jax.random.fold_in(key, 13)
    perm_keys = jax.random.split(key, TP_WAYS)
    return jax.vmap(lambda one_key: jax.random.permutation(one_key, CONTEXT_SPLITS))(perm_keys).astype(jnp.int32)


def place_ends(array, stream_key, least, top_value):
    place = [jax.random.randint(jax.random.fold_in(stream_key, axis), (), 0, length) for axis, length in enumerate(array.shape)]
    longest = array.shape.index(max(array.shape))
    beside = place[:longest] + [(place[longest] + 1) % array.shape[longest]] + place[longest + 1:]
    return array.at[tuple(place)].set(least).at[tuple(beside)].set(top_value)


def steps_of(stream_key, dims, shards, least, top_value):
    def one(position, shards_of):
        steps = jax.random.uniform(jax.random.fold_in(jax.random.fold_in(stream_key, 6), position), (shards_of,), jnp.float32, least / len(shards), top_value / len(shards))
        return jnp.repeat(jnp.exp(steps), dims[position] // shards_of).reshape((-1,) + (1,) * (len(dims) - position - 1))

    loudness = one(*shards[0])
    for cut in shards[1:]:
        loudness = loudness * one(*cut)
    return loudness


def bell_draw(key, dims, deviation, limit, cuts=(), kind=jnp.bfloat16):
    values = deviation * jax.random.normal(key, dims, jnp.float32)
    if cuts:
        values = values * steps_of(key, dims, cuts, -0.22, 0.18)
    return jnp.clip(values, -limit, limit).astype(kind)


def setup_inputs(seed: int = 0) -> dict:
    streams_of = jax.random.split(jax.random.key(seed), 14)
    return {
        "step_inputs": draw_step_inputs(jax.random.fold_in(streams_of[13], 71), 0),
        "attn_gain": jnp.clip(1.0 + 0.1 * jax.random.normal(streams_of[1], (D,), jnp.float32), 0.5, 1.5).astype(jnp.bfloat16),
        "mlp_gain": jnp.clip(1.0 + 0.1 * jax.random.normal(streams_of[2], (D,), jnp.float32), 0.5, 1.5).astype(jnp.bfloat16),
        "qkv_trainer": bell_draw(streams_of[3], (D, QKV_COLS), D ** -0.5, 0.0625, ((1, 128),)),
        "o_trainer": bell_draw(streams_of[4], (QUERY_HEADS * HEAD_SIZE, D), HEAD_SIZE ** -0.5, 0.5, ((0, 128),)),
        "gate_trainer": bell_draw(streams_of[5], (D, FF), D ** -0.5, 0.0625, ((1, 128),)),
        "up_trainer": bell_draw(streams_of[6], (D, FF), D ** -0.5, 0.0625, ((1, 128),)),
        "down_trainer": bell_draw(streams_of[7], (FF, D), FF ** -0.5, 0.03125, ((0, 128),)),
        "key_page_pool": draw_key_page_pool(jax.random.fold_in(streams_of[13], 71), 0),
        "value_page_pool": bell_draw(streams_of[9], (CONTEXT_SPLITS * SLOTS_PER_SPLIT, PAGE_TOKENS, KEY_VALUE_HEADS * HEAD_SIZE), 1.0, 6.0, ((0, 16), (2, 8))),
        "page_table": draw_page_table(jax.random.fold_in(streams_of[13], 71), 0),
        "lengths": place_ends(jax.random.randint(streams_of[11], (RESPONSE_BATCH,), 1, RESPONSE_LENGTH - 1), jax.random.fold_in(streams_of[11], 1), 1, (RESPONSE_LENGTH - 1) - 1).astype(jnp.int32),
        "shard_map": draw_shard_map(jax.random.fold_in(streams_of[13], 71), 0),
    }


norm_eps = 1e-05
rope_base = 500000.0
neg_large = -1e+30

def rotate(vectors, positions):
    half_dim = vectors.shape[-1] // 2
    frequency = jnp.power(jnp.float32(rope_base), -jnp.arange(half_dim, dtype=jnp.float32) * 2.0 / vectors.shape[-1])
    angles = positions[:, None] * frequency[None, :]
    angles = angles.reshape((angles.shape[0],) + (1,) * (vectors.ndim - 2) + (half_dim,))
    cosine = jnp.cos(angles)
    sine = jnp.sin(angles)
    front = vectors[..., :half_dim]
    back = vectors[..., half_dim:]
    return jnp.concatenate([front * cosine - back * sine, back * cosine + front * sine], axis=-1)

def rms_scale(values, square_sum, gain):
    return values * lax.rsqrt(square_sum[:, None] / D + norm_eps) * gain.astype(jnp.float32)[None, :]

def reference(step_inputs, attn_gain, mlp_gain, qkv_trainer, o_trainer, gate_trainer, up_trainer, down_trainer, key_page_pool, value_page_pool, page_table, lengths, shard_map):
    ctx_ids = jnp.arange(CONTEXT_SPLITS, dtype=jnp.int32)
    matches = shard_map[:, None, :] == ctx_ids[None, :, None]
    source_order = lax.optimization_barrier(jnp.sum(jnp.where(matches, ctx_ids[None, None, :], 0), axis=2)).astype(jnp.int32)
    head_index = jnp.arange(TP_WAYS, dtype=jnp.int32)[:, None]

    def logical_columns(stored):
        row_count, col_count = stored.shape
        block_cols = col_count // (TP_WAYS * CONTEXT_SPLITS)
        divided_view = stored.reshape(row_count, TP_WAYS, CONTEXT_SPLITS, block_cols)
        return divided_view[:, head_index, source_order].reshape(row_count, col_count)

    def logical_rows(stored):
        row_count, col_count = stored.shape
        block_rows = row_count // (TP_WAYS * CONTEXT_SPLITS)
        divided_view = stored.reshape(TP_WAYS, CONTEXT_SPLITS, block_rows, col_count)
        return divided_view[head_index, source_order].reshape(row_count, col_count)
    qkv_weight = logical_columns(qkv_trainer)
    gate_weight = logical_columns(gate_trainer)
    up_weight = logical_columns(up_trainer)
    o_weight = logical_rows(o_trainer)
    down_weight = logical_rows(down_trainer)
    heads_per_group = QUERY_HEADS // KEY_VALUE_HEADS
    scale = HEAD_SIZE ** (-0.5)
    block_ids = jnp.arange(BLOCKS, dtype=jnp.int32)
    global_slots = ((block_ids % CONTEXT_SPLITS)[None, :] * SLOTS_PER_SPLIT + page_table).astype(jnp.int32)
    cache_positions = jnp.arange(RESPONSE_LENGTH, dtype=jnp.int32)
    new_keys = []
    new_values = []
    results = []
    for step_index in range(STEPS):
        inputs_f = step_inputs[step_index].astype(jnp.float32)
        normed = rms_scale(inputs_f, lax.optimization_barrier(jnp.sum(inputs_f * inputs_f, axis=1)), attn_gain).astype(jnp.bfloat16)
        projected_rows = jnp.dot(normed, qkv_weight, preferred_element_type=jnp.float32)
        divided_view = projected_rows.reshape(RESPONSE_BATCH, KEY_VALUE_HEADS, heads_per_group + 2, HEAD_SIZE)
        positions_now = (lengths + step_index).astype(jnp.float32)
        queries = lax.optimization_barrier(rotate(divided_view[:, :, :heads_per_group], positions_now).astype(jnp.bfloat16))
        new_keys.append(lax.optimization_barrier(rotate(divided_view[:, :, heads_per_group], positions_now).astype(jnp.bfloat16)))
        new_values.append(lax.optimization_barrier(divided_view[:, :, heads_per_group + 1].astype(jnp.bfloat16)))
        key_stack = jnp.stack(new_keys, axis=1)
        value_stack = jnp.stack(new_values, axis=1)

        def attend(items):
            query_one, keys_one, values_one, slot_entry_row, length_one = items
            paged_keys = key_page_pool[slot_entry_row].reshape(RESPONSE_LENGTH, KEY_VALUE_HEADS, HEAD_SIZE)
            paged_values = value_page_pool[slot_entry_row].reshape(RESPONSE_LENGTH, KEY_VALUE_HEADS, HEAD_SIZE)
            all_keys = jnp.concatenate([paged_keys, keys_one], axis=0).astype(jnp.float32)
            all_values = jnp.concatenate([paged_values, values_one], axis=0).astype(jnp.float32)
            live_mask = jnp.concatenate([cache_positions < length_one, jnp.ones((keys_one.shape[0],), dtype=bool)])
            scores = jnp.einsum('gqd,kgd->gqk', query_one.astype(jnp.float32), all_keys, precision=lax.Precision.HIGHEST) * scale
            masked = jnp.where(live_mask[None, None, :], scores, neg_large)
            top_score = lax.optimization_barrier(jnp.max(masked, axis=-1, keepdims=True))
            weights = jnp.where(live_mask[None, None, :], jnp.exp(masked - top_score), 0.0)
            weight_sum = lax.optimization_barrier(jnp.sum(weights, axis=-1))
            rounded = lax.optimization_barrier(weights.astype(jnp.bfloat16)).astype(jnp.float32)
            summed = jnp.einsum('gqk,kgd->gqd', rounded, all_values, precision=lax.Precision.HIGHEST)
            return (summed / weight_sum[..., None]).astype(jnp.bfloat16)
        attended = lax.map(attend, (queries, key_stack, value_stack, global_slots, lengths)).reshape(RESPONSE_BATCH, QUERY_HEADS * HEAD_SIZE)
        residual = inputs_f + jnp.dot(attended, o_weight, preferred_element_type=jnp.float32)
        mlp_in = rms_scale(residual, lax.optimization_barrier(jnp.sum(residual * residual, axis=1)), mlp_gain).astype(jnp.bfloat16)
        gate_val = jnp.dot(mlp_in, gate_weight, preferred_element_type=jnp.float32)
        up_val = jnp.dot(mlp_in, up_weight, preferred_element_type=jnp.float32)
        hidden = (jax.nn.silu(gate_val) * up_val).astype(jnp.bfloat16)
        layer_out = residual + jnp.dot(hidden, down_weight, preferred_element_type=jnp.float32)
        results.append(layer_out.astype(jnp.bfloat16))
    return jnp.stack(results, axis=0)
```

```python
import functools

import jax
import jax.numpy as jnp
import numpy as np
from jax import lax
from jax.experimental import pallas as pl
from jax.experimental.pallas import tpu as pltpu
from jax.sharding import PartitionSpec as P

D = 8192
HEAD_SIZE = 128
STEPS = 2
RESPONSES = 8
ROWS = STEPS * RESPONSES
HEADS = 8
CTX = 16
HEAD = 8
WIDTH = D // CTX
QKV = 80
OUT_ROWS = 64
HIDDEN = 224
PAGES = 16
PAGE = 128
MESSAGE = WIDTH + 128
NORM_EPS = 1e-05
ROPE_BASE = 500000.0
NEG = -1e30
F32 = jnp.float32
BF16 = jnp.bfloat16
MESH = pl.DeviceIdType.MESH

HOPS_Y = {0: 0, 1: 1, 2: 2, 3: 1}


def hops(k):
    return HOPS_Y[k // 4] + (k // 2) % 2


NEAR = sorted(range(1, CTX), key=lambda k: (hops(k), k % 2, k))
FAR = NEAR[::-1]

NT = (((1,), (1,)), ((), ()))


def frequency_table():
    half = HEAD_SIZE // 2
    f = ROPE_BASE ** (-np.arange(half, dtype=np.float64) * 2.0 / HEAD_SIZE)
    row = np.concatenate([f, f]).astype(np.float32)
    return np.broadcast_to(row[None, :], (8, HEAD_SIZE)).copy()


def split_sum(ssq):
    hi = ssq.astype(BF16).astype(F32)
    mid = (ssq - hi).astype(BF16).astype(F32)
    lo = ((ssq - hi) - mid).astype(BF16).astype(F32)
    lane = lax.broadcasted_iota(jnp.int32, (ROWS, 128), 1)
    tile = jnp.where(lane == 0, hi, jnp.where(lane == 1, mid, jnp.where(lane == 2, lo, 0.0)))
    return tile.astype(BF16)


def kernel(
    x_hbm, ag_hbm, mg_hbm, qkv_hbm, o_hbm, gate_hbm, up_hbm, down_hbm, k_hbm, v_hbm,
    pt_hbm, len_hbm, sm_hbm, f_hbm,
    out_ref,
    x_v, ag_v, mg_v, f_v, pt_s, len_s, sm_s, inv_s,
    qkv_w, o_w, gate_w, up_w, down_w, k_w, v_w,
    a_buf, b_send, b_buf, qs, kn, vn, osc, mls, c_send, c_buf,
    d1_send, d1_buf, d2_send, d2_buf, d3_buf, e1_send, e1_buf, e2_send, e2_buf, res_v,
    small_sem, load_sem, send_sem, recv_sem, a_sem, d3_sem,
):
    h = lax.axis_index("head")
    c = lax.axis_index("ctx")
    h_step = [(1 << i) * (1 - 2 * ((h // (1 << i)) % 2)) for i in range(3)]
    c_step = [(1 << i) * (1 - 2 * ((c // (1 << i)) % 2)) for i in range(4)]

    def ctx_of(k):
        out = c
        for i in range(4):
            if (k >> i) & 1:
                out = out + c_step[i]
        return out

    def head_of(k):
        out = h
        for i in range(3):
            if (k >> i) & 1:
                out = out + h_step[i]
        return out

    def same(k):
        return (h, ctx_of(k))

    def cross(k):
        return (h + h_step[0] if k & 2 else h, ctx_of(k))

    barrier = pltpu.get_barrier_semaphore()
    partners = [same(k) for k in range(1, CTX)]
    partners += [cross(k) for k in range(1, CTX) if k & 2]
    partners += [(head_of(k), c) for k in range(1, HEAD)]
    for partner in partners:
        pl.semaphore_signal(barrier, inc=1, device_id=partner, device_id_type=MESH)

    small = [(x_hbm, x_v), (ag_hbm, ag_v), (mg_hbm, mg_v), (f_hbm, f_v), (pt_hbm, pt_s), (len_hbm, len_s), (sm_hbm, sm_s)]
    small = [pltpu.make_async_copy(src, dst, small_sem.at[i]) for i, (src, dst) in enumerate(small)]
    for copy in small:
        copy.start()
    large = [(qkv_hbm, qkv_w), (k_hbm, k_w), (v_hbm, v_w), (o_hbm, o_w), (gate_hbm, gate_w), (up_hbm, up_w), (down_hbm, down_w)]
    large = [pltpu.make_async_copy(src, dst, load_sem.at[i]) for i, (src, dst) in enumerate(large)]
    for copy in large:
        copy.start()
    load_qkv, load_k, load_v, load_o, load_gate, load_up, load_down = large
    for copy in small:
        copy.wait()

    x_f = jnp.concatenate([x_v[0].astype(F32), x_v[1].astype(F32)], axis=0)
    a_buf[0, :, :WIDTH] = (x_f * ag_v[...].astype(F32)[None, :]).astype(BF16)
    a_buf[0, :, WIDTH:] = split_sum(jnp.sum(x_f * x_f, axis=1, keepdims=True))

    row = lax.broadcasted_iota(jnp.int32, (ROWS, 128), 0)
    lane = lax.broadcasted_iota(jnp.int32, (ROWS, 128), 1)
    position = jnp.zeros((ROWS, 128), jnp.int32)
    for i in range(ROWS):
        position = jnp.where(row == i, len_s[i % RESPONSES] + i // RESPONSES, position)
    angle = position.astype(F32) * f_v[0:1, :]
    cosine = jnp.cos(angle)
    sine = jnp.sin(angle)
    sine = jnp.where(lane < HEAD_SIZE // 2, -sine, sine)

    for j in range(CTX):
        total = jnp.int32(0)
        for i in range(CTX):
            total = total + jnp.where(sm_s[0, i] == j, jnp.int32(i), jnp.int32(0))
        inv_s[j] = total

    pl.semaphore_wait(barrier, len(partners))

    def exchange(phase, pairs):
        for src, dst, partner in pairs:
            pltpu.make_async_remote_copy(
                src_ref=src, dst_ref=dst, send_sem=send_sem.at[phase], recv_sem=recv_sem.at[phase],
                device_id=partner, device_id_type=MESH,
            ).start()

    def arrived(phase, ref):
        pltpu.make_async_copy(ref, ref, recv_sem.at[phase]).wait()

    def sent(phase, ref):
        pltpu.make_async_copy(ref, ref, send_sem.at[phase]).wait()

    def gather_start(phase, buf, sems):
        for k in FAR:
            pltpu.make_async_remote_copy(
                src_ref=buf.at[0], dst_ref=buf.at[k], send_sem=send_sem.at[phase], recv_sem=sems.at[k],
                device_id=cross(k), device_id_type=MESH,
            ).start()

    def gather_wait(buf, sems, k):
        pltpu.make_async_copy(buf.at[k], buf.at[k], sems.at[k]).wait()

    def row_scale(squares):
        total = jnp.sum(squares, axis=1, keepdims=True)
        return lax.rsqrt(total / D + NORM_EPS)

    gather_start(0, a_buf, a_sem)
    load_qkv.wait()
    projected = jnp.zeros((ROWS, QKV), F32)
    squares = jnp.zeros((ROWS, 128), F32)
    for k in [0] + NEAR:
        if k:
            gather_wait(a_buf, a_sem, k)
        columns = pl.ds(pl.multiple_of(ctx_of(k) * WIDTH, WIDTH), WIDTH)
        projected += lax.dot_general(a_buf[k, :, :WIDTH], qkv_w[:, columns], NT, preferred_element_type=F32)
        squares += a_buf[k, :, WIDTH:].astype(F32)
    projected = projected * row_scale(squares)

    b_send[...] = jnp.zeros((ROWS, 128), F32)
    b_send[:, :QKV] = projected
    exchange(1, [(b_send, b_buf.at[k], same(k)) for k in FAR])
    b_buf[0] = b_send[...]
    arrived(1, b_buf.at[pl.ds(1, CTX - 1)])

    def slot_of(other):
        slot = jnp.int32(0)
        for i in range(4):
            bit = 1 << i
            slot = slot + bit * ((c // bit + other // bit) % 2)
        return slot

    blocks = [b_buf[slot_of(inv_s[j])] for j in range(CTX)]

    def head_tile(t):
        out = jnp.zeros((ROWS, 128), F32)
        for j in range(CTX):
            start = QKV * j - 128 * t
            if start >= 128 or start + QKV <= 0:
                continue
            piece = blocks[j] if start == 0 else pltpu.roll(blocks[j], start % 128, 1)
            out = jnp.where((lane >= start) & (lane < start + QKV), piece, out)
        return out

    def rope(tile):
        return tile * cosine + pltpu.roll(tile, HEAD_SIZE // 2, 1) * sine

    for t in range(HEADS):
        qs[:, t, :] = rope(head_tile(t))
    kn[...] = jnp.zeros_like(kn)
    vn[...] = jnp.zeros_like(vn)
    kn[:ROWS, :] = rope(head_tile(HEADS)).astype(BF16)
    vn[:ROWS, :] = head_tile(HEADS + 1).astype(BF16)

    load_k.wait()
    load_v.wait()
    scale = HEAD_SIZE ** (-0.5)
    lane2 = lax.broadcasted_iota(jnp.int32, (ROWS, 2 * PAGE), 1)
    for r in range(RESPONSES):
        q = jnp.concatenate([qs[r], qs[RESPONSES + r]], axis=0).astype(BF16)
        pages = [pt_s[r, j * CTX + c] for j in range(PAGES)]
        scores = []
        for j in range(0, PAGES, 2):
            keys = jnp.concatenate([k_w[pages[j]], k_w[pages[j + 1]]], axis=0)
            s = lax.dot_general(q, keys, NT, preferred_element_type=F32) * scale
            offset = (j * CTX + c) * PAGE
            place = offset + lane2 + jnp.where(lane2 >= PAGE, (CTX - 1) * PAGE, 0)
            scores.append((s, place < len_s[r]))
        s = lax.dot_general(q, kn[...], NT, preferred_element_type=F32) * scale
        live = (lane < ROWS) & (lane % RESPONSES == r) & (lane // RESPONSES <= row // HEADS) & (c == 0)
        scores.append((s, live))
        masked = [jnp.where(live, s, NEG) for s, live in scores]
        top = jnp.max(masked[-1], axis=1, keepdims=True)
        wide = masked[0]
        for s in masked[1:-1]:
            wide = jnp.maximum(wide, s)
        top = jnp.maximum(top, jnp.max(wide, axis=1, keepdims=True))
        weights = [jnp.where(live, jnp.exp(s - top), 0.0) for s, (_, live) in zip(masked, scores, strict=True)]
        wide = weights[0]
        for w in weights[1:-1]:
            wide = wide + w
        total = jnp.sum(weights[-1], axis=1, keepdims=True) + jnp.sum(wide, axis=1, keepdims=True)
        out = jnp.dot(weights[-1].astype(BF16), vn[...], preferred_element_type=F32)
        for j in range(0, PAGES, 2):
            values = jnp.concatenate([v_w[pages[j]], v_w[pages[j + 1]]], axis=0)
            out += jnp.dot(weights[j // 2].astype(BF16), values, preferred_element_type=F32)
        both = jnp.where(lane < 96, top, total)
        for s in range(STEPS):
            osc[:, s * RESPONSES + r, :] = out[s * HEADS : (s + 1) * HEADS]
            mls[:, s * RESPONSES + r, :] = both[s * HEADS : (s + 1) * HEADS]

    def half_head(k):
        block = sm_s[0, ctx_of(k)]
        values = osc[block // 2]
        values = jnp.where(block % 2 == 1, pltpu.roll(values, HEAD_SIZE // 2, 1), values)
        return jnp.where(lane < HEAD_SIZE // 2, values, mls[block // 2])

    for k in FAR:
        c_send[k] = half_head(k)
        exchange(2, [(c_send.at[k], c_buf.at[k], same(k))])
    c_buf[0] = half_head(0)
    arrived(2, c_buf.at[pl.ds(1, CTX - 1)])
    parts = [c_buf[k] for k in range(CTX)]
    tops = [p[:, 64:65] for p in parts]
    top = functools.reduce(jnp.maximum, tops)
    total = jnp.zeros((ROWS, 1), F32)
    out = jnp.zeros((ROWS, 128), F32)
    for p, t in zip(parts, tops, strict=True):
        factor = jnp.exp(t - top)
        total = total + factor * p[:, 96:97]
        out = out + factor * p
    attended = (out / total).astype(BF16)[:, :OUT_ROWS]

    def reduce_scatter(phase, left, weight, send, buf):
        for k in FAR + [0]:
            columns = pl.ds(pl.multiple_of(ctx_of(k) * WIDTH, WIDTH), WIDTH)
            block = jnp.dot(left, weight[:, columns], preferred_element_type=F32)
            if k:
                send[k] = block.astype(BF16)
                exchange(phase, [(send.at[k], buf.at[k], cross(k))])
        arrived(phase, buf.at[pl.ds(1, CTX - 1)])
        for k in range(1, CTX):
            block = block + buf[k].astype(F32)
        return block

    def sum_over_head(phase, block, send, buf):
        send[...] = block.astype(send.dtype)
        exchange(phase, [(send, buf.at[k], (head_of(k), c)) for k in range(HEAD - 1, 0, -1)])
        buf[0] = send[...]
        arrived(phase, buf.at[pl.ds(1, HEAD - 1)])
        total = None
        for other in range(HEAD):
            slot = jnp.int32(0)
            for i in range(3):
                bit = 1 << i
                slot = slot + bit * ((h // bit + other // bit) % 2)
            term = buf[slot].astype(F32)
            total = term if total is None else total + term
        return total

    load_o.wait()
    block = reduce_scatter(3, attended, o_w, d1_send, d1_buf)
    x_f = jnp.concatenate([x_v[0].astype(F32), x_v[1].astype(F32)], axis=0)
    residual = x_f + sum_over_head(4, block, d2_send, d2_buf)
    res_v[...] = residual
    d3_buf[0, :, :WIDTH] = (residual * mg_v[...].astype(F32)[None, :]).astype(BF16)
    d3_buf[0, :, WIDTH:] = split_sum(jnp.sum(residual * residual, axis=1, keepdims=True))
    gather_start(5, d3_buf, d3_sem)
    load_gate.wait()
    load_up.wait()
    gate = jnp.zeros((ROWS, HIDDEN), F32)
    up = jnp.zeros((ROWS, HIDDEN), F32)
    squares = jnp.zeros((ROWS, 128), F32)
    for k in [0] + NEAR:
        if k:
            gather_wait(d3_buf, d3_sem, k)
        columns = pl.ds(pl.multiple_of(ctx_of(k) * WIDTH, WIDTH), WIDTH)
        left = d3_buf[k, :, :WIDTH]
        gate += lax.dot_general(left, gate_w[:, columns], NT, preferred_element_type=F32)
        up += lax.dot_general(left, up_w[:, columns], NT, preferred_element_type=F32)
        squares += d3_buf[k, :, WIDTH:].astype(F32)
    rms = row_scale(squares)
    gate = gate * rms
    up = up * rms
    hidden = (gate / (1.0 + jnp.exp(-gate)) * up).astype(BF16)

    load_down.wait()
    block = reduce_scatter(6, hidden, down_w, e1_send, e1_buf)
    decoded = res_v[...] + sum_over_head(7, block, e2_send, e2_buf)
    out_ref[0] = decoded[:RESPONSES].astype(BF16)
    out_ref[1] = decoded[RESPONSES:].astype(BF16)

    sent(0, a_buf.at[pl.ds(1, CTX - 1)])
    sent(1, b_buf.at[pl.ds(1, CTX - 1)])
    sent(2, c_buf.at[pl.ds(1, CTX - 1)])
    sent(3, d1_buf.at[pl.ds(1, CTX - 1)])
    sent(4, d2_buf.at[pl.ds(1, HEAD - 1)])
    sent(5, d3_buf.at[pl.ds(1, CTX - 1)])
    sent(6, e1_buf.at[pl.ds(1, CTX - 1)])
    sent(7, e2_buf.at[pl.ds(1, HEAD - 1)])


HEAD_SUM = BF16


def body(
    step_inputs, attn_gain, mlp_gain, qkv_trainer, o_trainer, gate_trainer, up_trainer, down_trainer,
    key_page_pool, value_page_pool, page_table, lengths, shard_map,
):
    operands = (
        step_inputs, attn_gain, mlp_gain, qkv_trainer.T, o_trainer, gate_trainer.T, up_trainer.T, down_trainer,
        key_page_pool, value_page_pool, page_table, lengths, shard_map, jnp.asarray(frequency_table()),
    )
    vmem, smem = pltpu.VMEM, pltpu.SMEM
    scratch = [
        vmem((STEPS, RESPONSES, WIDTH), BF16), vmem((WIDTH,), BF16), vmem((WIDTH,), BF16), vmem((8, HEAD_SIZE), F32),
        smem(page_table.shape, jnp.int32), smem((RESPONSES,), jnp.int32), smem((1, CTX), jnp.int32), smem((CTX,), jnp.int32),
        vmem((QKV, D), BF16), vmem((OUT_ROWS, D), BF16), vmem((HIDDEN, D), BF16), vmem((HIDDEN, D), BF16), vmem((HIDDEN, D), BF16),
        vmem(key_page_pool.shape, BF16), vmem(value_page_pool.shape, BF16),
        vmem((CTX, ROWS, MESSAGE), BF16), vmem((ROWS, 128), F32), vmem((CTX, ROWS, 128), F32),
        vmem((ROWS, HEADS, 128), F32), vmem((128, 128), BF16), vmem((128, 128), BF16),
        vmem((HEADS, ROWS, 128), F32), vmem((HEADS, ROWS, 128), F32),
        vmem((CTX, ROWS, 128), F32), vmem((CTX, ROWS, 128), F32),
        vmem((CTX, ROWS, WIDTH), BF16), vmem((CTX, ROWS, WIDTH), BF16), vmem((ROWS, WIDTH), HEAD_SUM), vmem((HEAD, ROWS, WIDTH), HEAD_SUM),
        vmem((CTX, ROWS, MESSAGE), BF16),
        vmem((CTX, ROWS, WIDTH), BF16), vmem((CTX, ROWS, WIDTH), BF16), vmem((ROWS, WIDTH), HEAD_SUM), vmem((HEAD, ROWS, WIDTH), HEAD_SUM),
        vmem((ROWS, WIDTH), F32),
        pltpu.SemaphoreType.DMA((7,)), pltpu.SemaphoreType.DMA((7,)), pltpu.SemaphoreType.DMA((8,)), pltpu.SemaphoreType.DMA((8,)),
        pltpu.SemaphoreType.DMA((CTX,)), pltpu.SemaphoreType.DMA((CTX,)),
    ]
    return pl.pallas_call(
        kernel,
        out_shape=jax.ShapeDtypeStruct((STEPS, RESPONSES, WIDTH), BF16),
        in_specs=[pl.BlockSpec(memory_space=pl.ANY)] * len(operands),
        out_specs=pl.BlockSpec(memory_space=pltpu.VMEM),
        scratch_shapes=scratch,
        compiler_params=pltpu.CompilerParams(
            collective_id=0, has_side_effects=True, vmem_limit_bytes=60 * 1024 * 1024
        ),
    )(*operands)


def solution(mesh):
    in_specs = (
        P(None, None, "ctx"),
        P("ctx"),
        P("ctx"),
        P(None, ("head", "ctx")),
        P(("head", "ctx"), None),
        P(None, ("head", "ctx")),
        P(None, ("head", "ctx")),
        P(("head", "ctx"), None),
        P("ctx", None, "head"),
        P("ctx", None, "head"),
        P(),
        P(),
        P("head", None),
    )
    out_specs = P(None, None, "ctx")
    return jax.shard_map(body, mesh=mesh, in_specs=in_specs, out_specs=out_specs, check_vma=False)
```

```python
import functools

import jax
import jax.numpy as jnp
import numpy as np
from jax import lax
from jax.experimental import pallas as pl
from jax.experimental.pallas import tpu as pltpu
from jax.sharding import PartitionSpec as P

D = 8192
HEAD_SIZE = 128
STEPS = 2
RESPONSES = 8
ROWS = STEPS * RESPONSES
HEADS = 8
CTX = 16
HEAD = 8
WIDTH = D // CTX
QKV = 80
OUT_ROWS = 64
HIDDEN = 224
PAGES = 16
PAGE = 128
MESSAGE = WIDTH + 128
NORM_EPS = 1e-05
ROPE_BASE = 500000.0
NEG = -1e30
F32 = jnp.float32
BF16 = jnp.bfloat16
MESH = pl.DeviceIdType.MESH

HOPS_Y = {0: 0, 1: 1, 2: 2, 3: 1}


def hops(k):
    return HOPS_Y[k // 4] + (k // 2) % 2


NEAR = sorted(range(1, CTX), key=lambda k: (hops(k), k % 2, k))
FAR = NEAR[::-1]

NT = (((1,), (1,)), ((), ()))


def frequency_table():
    half = HEAD_SIZE // 2
    f = ROPE_BASE ** (-np.arange(half, dtype=np.float64) * 2.0 / HEAD_SIZE)
    row = np.concatenate([f, f]).astype(np.float32)
    return np.broadcast_to(row[None, :], (8, HEAD_SIZE)).copy()


def split_sum(ssq):
    hi = ssq.astype(BF16).astype(F32)
    mid = (ssq - hi).astype(BF16).astype(F32)
    lo = ((ssq - hi) - mid).astype(BF16).astype(F32)
    lane = lax.broadcasted_iota(jnp.int32, (ROWS, 128), 1)
    tile = jnp.where(lane == 0, hi, jnp.where(lane == 1, mid, jnp.where(lane == 2, lo, 0.0)))
    return tile.astype(BF16)


def kernel(
    x_hbm, ag_hbm, mg_hbm, qkv_hbm, o_hbm, gate_hbm, up_hbm, down_hbm, k_hbm, v_hbm,
    pt_hbm, len_hbm, sm_hbm, f_hbm,
    out_ref,
    x_v, ag_v, mg_v, f_v, pt_s, len_s, sm_s, inv_s,
    qkv_w, o_w, gate_w, up_w, down_w, k_w, v_w,
    a_buf, b_send, b_buf, qs, kn, vn, osc, mls, c_send, c_buf,
    d1_send, d1_buf, d2_send, d2_buf, d3_buf, e1_send, e1_buf, e2_send, e2_buf, res_v,
    small_sem, load_sem, send_sem, recv_sem, a_sem, d3_sem,
):
    h = lax.axis_index("head")
    c = lax.axis_index("ctx")
    h_step = [(1 << i) * (1 - 2 * ((h // (1 << i)) % 2)) for i in range(3)]
    c_step = [(1 << i) * (1 - 2 * ((c // (1 << i)) % 2)) for i in range(4)]

    def ctx_of(k):
        out = c
        for i in range(4):
            if (k >> i) & 1:
                out = out + c_step[i]
        return out

    def head_of(k):
        out = h
        for i in range(3):
            if (k >> i) & 1:
                out = out + h_step[i]
        return out

    def same(k):
        return (h, ctx_of(k))

    def cross(k):
        return (h + h_step[0] if k & 2 else h, ctx_of(k))

    barrier = pltpu.get_barrier_semaphore()
    partners = [same(k) for k in range(1, CTX)]
    partners += [cross(k) for k in range(1, CTX) if k & 2]
    partners += [(head_of(k), c) for k in range(1, HEAD)]
    for partner in partners:
        pl.semaphore_signal(barrier, inc=1, device_id=partner, device_id_type=MESH)

    small = [(x_hbm, x_v), (ag_hbm, ag_v), (mg_hbm, mg_v), (f_hbm, f_v), (pt_hbm, pt_s), (len_hbm, len_s), (sm_hbm, sm_s)]
    small = [pltpu.make_async_copy(src, dst, small_sem.at[i]) for i, (src, dst) in enumerate(small)]
    for copy in small:
        copy.start()
    large = [(qkv_hbm, qkv_w), (k_hbm, k_w), (v_hbm, v_w), (o_hbm, o_w), (gate_hbm, gate_w), (up_hbm, up_w), (down_hbm, down_w)]
    large = [pltpu.make_async_copy(src, dst, load_sem.at[i]) for i, (src, dst) in enumerate(large)]
    for copy in large:
        copy.start()
    load_qkv, load_k, load_v, load_o, load_gate, load_up, load_down = large
    for copy in small:
        copy.wait()

    row = lax.broadcasted_iota(jnp.int32, (ROWS, 128), 0)
    lane = lax.broadcasted_iota(jnp.int32, (ROWS, 128), 1)

    x_f = jnp.concatenate([x_v[0].astype(F32), x_v[1].astype(F32)], axis=0)
    gains = ag_v[...].astype(F32)[None, :]
    tile = jnp.zeros((ROWS, 128), F32)
    for i in range(WIDTH // 128):
        tile = jnp.where(row == i, gains[:, 128 * i : 128 * (i + 1)], tile)
    a_buf[0, :, :WIDTH] = x_f.astype(BF16)
    a_buf[0, :, WIDTH:] = tile.astype(BF16)

    position = jnp.zeros((ROWS, 128), jnp.int32)
    for i in range(ROWS):
        position = jnp.where(row == i, len_s[i % RESPONSES] + i // RESPONSES, position)
    angle = position.astype(F32) * f_v[0:1, :]
    cosine = jnp.cos(angle)
    sine = jnp.sin(angle)
    sine = jnp.where(lane < HEAD_SIZE // 2, -sine, sine)

    for j in range(CTX):
        total = jnp.int32(0)
        for i in range(CTX):
            total = total + jnp.where(sm_s[0, i] == j, jnp.int32(i), jnp.int32(0))
        inv_s[j] = total

    pl.semaphore_wait(barrier, len(partners))

    def exchange(phase, pairs):
        for src, dst, partner in pairs:
            pltpu.make_async_remote_copy(
                src_ref=src, dst_ref=dst, send_sem=send_sem.at[phase], recv_sem=recv_sem.at[phase],
                device_id=partner, device_id_type=MESH,
            ).start()

    def arrived(phase, ref):
        pltpu.make_async_copy(ref, ref, recv_sem.at[phase]).wait()

    def sent(phase, ref):
        pltpu.make_async_copy(ref, ref, send_sem.at[phase]).wait()

    def gather_start(phase, buf, sems):
        for k in FAR:
            pltpu.make_async_remote_copy(
                src_ref=buf.at[0], dst_ref=buf.at[k], send_sem=send_sem.at[phase], recv_sem=sems.at[k],
                device_id=cross(k), device_id_type=MESH,
            ).start()

    def gather_wait(buf, sems, k):
        pltpu.make_async_copy(buf.at[k], buf.at[k], sems.at[k]).wait()

    def row_scale(squares):
        total = jnp.sum(squares, axis=1, keepdims=True)
        return lax.rsqrt(total / D + NORM_EPS)

    gather_start(0, a_buf, a_sem)
    load_qkv.wait()
    squares = jnp.zeros((ROWS, 128), F32)
    for k in [0] + NEAR:
        if k:
            gather_wait(a_buf, a_sem, k)
        block = a_buf[k, :, :WIDTH].astype(F32)
        for i in range(WIDTH // 128):
            squares += block[:, 128 * i : 128 * (i + 1)] * block[:, 128 * i : 128 * (i + 1)]
    rms = row_scale(squares)
    projected = jnp.zeros((ROWS, QKV), F32)
    for k in range(CTX):
        gains = a_buf[k, :, WIDTH:].astype(F32)
        gains = jnp.concatenate([gains[i : i + 1] for i in range(WIDTH // 128)], axis=1)
        normed = (a_buf[k, :, :WIDTH].astype(F32) * rms * gains).astype(BF16)
        columns = pl.ds(pl.multiple_of(ctx_of(k) * WIDTH, WIDTH), WIDTH)
        projected += lax.dot_general(normed, qkv_w[:, columns], NT, preferred_element_type=F32)

    b_send[...] = jnp.zeros((ROWS, 128), F32)
    b_send[:, :QKV] = projected
    exchange(1, [(b_send, b_buf.at[k], same(k)) for k in FAR])
    b_buf[0] = b_send[...]
    arrived(1, b_buf.at[pl.ds(1, CTX - 1)])

    def slot_of(other):
        slot = jnp.int32(0)
        for i in range(4):
            bit = 1 << i
            slot = slot + bit * ((c // bit + other // bit) % 2)
        return slot

    blocks = [b_buf[slot_of(inv_s[j])] for j in range(CTX)]

    def head_tile(t):
        out = jnp.zeros((ROWS, 128), F32)
        for j in range(CTX):
            start = QKV * j - 128 * t
            if start >= 128 or start + QKV <= 0:
                continue
            piece = blocks[j] if start == 0 else pltpu.roll(blocks[j], start % 128, 1)
            out = jnp.where((lane >= start) & (lane < start + QKV), piece, out)
        return out

    def rope(tile):
        return tile * cosine + pltpu.roll(tile, HEAD_SIZE // 2, 1) * sine

    for t in range(HEADS):
        qs[:, t, :] = rope(head_tile(t))
    kn[...] = jnp.zeros_like(kn)
    vn[...] = jnp.zeros_like(vn)
    kn[:ROWS, :] = rope(head_tile(HEADS)).astype(BF16)
    vn[:ROWS, :] = head_tile(HEADS + 1).astype(BF16)

    load_k.wait()
    load_v.wait()
    scale = HEAD_SIZE ** (-0.5)
    lane2 = lax.broadcasted_iota(jnp.int32, (ROWS, 2 * PAGE), 1)
    for r in range(RESPONSES):
        q = jnp.concatenate([qs[r], qs[RESPONSES + r]], axis=0).astype(BF16)
        pages = [pt_s[r, j * CTX + c] for j in range(PAGES)]
        scores = []
        for j in range(0, PAGES, 2):
            keys = jnp.concatenate([k_w[pages[j]], k_w[pages[j + 1]]], axis=0)
            s = lax.dot_general(q, keys, NT, preferred_element_type=F32) * scale
            offset = (j * CTX + c) * PAGE
            place = offset + lane2 + jnp.where(lane2 >= PAGE, (CTX - 1) * PAGE, 0)
            scores.append((s, place < len_s[r]))
        s = lax.dot_general(q, kn[...], NT, preferred_element_type=F32) * scale
        live = (lane < ROWS) & (lane % RESPONSES == r) & (lane // RESPONSES <= row // HEADS) & (c == 0)
        scores.append((s, live))
        masked = [jnp.where(live, s, NEG) for s, live in scores]
        top = jnp.max(masked[-1], axis=1, keepdims=True)
        wide = masked[0]
        for s in masked[1:-1]:
            wide = jnp.maximum(wide, s)
        top = jnp.maximum(top, jnp.max(wide, axis=1, keepdims=True))
        weights = [jnp.where(live, jnp.exp(s - top), 0.0) for s, (_, live) in zip(masked, scores, strict=True)]
        wide = weights[0]
        for w in weights[1:-1]:
            wide = wide + w
        total = jnp.sum(weights[-1], axis=1, keepdims=True) + jnp.sum(wide, axis=1, keepdims=True)
        out = jnp.dot(weights[-1].astype(BF16), vn[...], preferred_element_type=F32)
        for j in range(0, PAGES, 2):
            values = jnp.concatenate([v_w[pages[j]], v_w[pages[j + 1]]], axis=0)
            out += jnp.dot(weights[j // 2].astype(BF16), values, preferred_element_type=F32)
        both = jnp.where(lane < 96, top, total)
        for s in range(STEPS):
            osc[:, s * RESPONSES + r, :] = out[s * HEADS : (s + 1) * HEADS]
            mls[:, s * RESPONSES + r, :] = both[s * HEADS : (s + 1) * HEADS]

    def half_head(k):
        block = sm_s[0, ctx_of(k)]
        values = osc[block // 2]
        values = jnp.where(block % 2 == 1, pltpu.roll(values, HEAD_SIZE // 2, 1), values)
        return jnp.where(lane < HEAD_SIZE // 2, values, mls[block // 2])

    for k in FAR:
        c_send[k] = half_head(k)
        exchange(2, [(c_send.at[k], c_buf.at[k], same(k))])
    c_buf[0] = half_head(0)
    arrived(2, c_buf.at[pl.ds(1, CTX - 1)])
    parts = [c_buf[k] for k in range(CTX)]
    tops = [p[:, 64:65] for p in parts]
    top = functools.reduce(jnp.maximum, tops)
    total = jnp.zeros((ROWS, 1), F32)
    out = jnp.zeros((ROWS, 128), F32)
    for p, t in zip(parts, tops, strict=True):
        factor = jnp.exp(t - top)
        total = total + factor * p[:, 96:97]
        out = out + factor * p
    attended = (out / total).astype(BF16)[:, :OUT_ROWS]

    def reduce_scatter(phase, left, weight, send, buf):
        for k in FAR + [0]:
            columns = pl.ds(pl.multiple_of(ctx_of(k) * WIDTH, WIDTH), WIDTH)
            block = jnp.dot(left, weight[:, columns], preferred_element_type=F32)
            if k:
                send[k] = block.astype(BF16)
                exchange(phase, [(send.at[k], buf.at[k], cross(k))])
        arrived(phase, buf.at[pl.ds(1, CTX - 1)])
        for k in range(1, CTX):
            block = block + buf[k].astype(F32)
        return block

    def sum_over_head(phase, block, send, buf):
        send[...] = block.astype(send.dtype)
        exchange(phase, [(send, buf.at[k], (head_of(k), c)) for k in range(HEAD - 1, 0, -1)])
        buf[0] = send[...]
        arrived(phase, buf.at[pl.ds(1, HEAD - 1)])
        total = None
        for other in range(HEAD):
            slot = jnp.int32(0)
            for i in range(3):
                bit = 1 << i
                slot = slot + bit * ((h // bit + other // bit) % 2)
            term = buf[slot].astype(F32)
            total = term if total is None else total + term
        return total

    load_o.wait()
    block = reduce_scatter(3, attended, o_w, d1_send, d1_buf)
    x_f = jnp.concatenate([x_v[0].astype(F32), x_v[1].astype(F32)], axis=0)
    residual = x_f + sum_over_head(4, block, d2_send, d2_buf)
    res_v[...] = residual
    d3_buf[0, :, :WIDTH] = (residual * mg_v[...].astype(F32)[None, :]).astype(BF16)
    d3_buf[0, :, WIDTH:] = split_sum(jnp.sum(residual * residual, axis=1, keepdims=True))
    gather_start(5, d3_buf, d3_sem)
    load_gate.wait()
    load_up.wait()
    gate = jnp.zeros((ROWS, HIDDEN), F32)
    up = jnp.zeros((ROWS, HIDDEN), F32)
    squares = jnp.zeros((ROWS, 128), F32)
    for k in [0] + NEAR:
        if k:
            gather_wait(d3_buf, d3_sem, k)
        columns = pl.ds(pl.multiple_of(ctx_of(k) * WIDTH, WIDTH), WIDTH)
        left = d3_buf[k, :, :WIDTH]
        gate += lax.dot_general(left, gate_w[:, columns], NT, preferred_element_type=F32)
        up += lax.dot_general(left, up_w[:, columns], NT, preferred_element_type=F32)
        squares += d3_buf[k, :, WIDTH:].astype(F32)
    rms = row_scale(squares)
    gate = gate * rms
    up = up * rms
    hidden = (gate / (1.0 + jnp.exp(-gate)) * up).astype(BF16)

    load_down.wait()
    block = reduce_scatter(6, hidden, down_w, e1_send, e1_buf)
    decoded = res_v[...] + sum_over_head(7, block, e2_send, e2_buf)
    out_ref[0] = decoded[:RESPONSES].astype(BF16)
    out_ref[1] = decoded[RESPONSES:].astype(BF16)

    sent(0, a_buf.at[pl.ds(1, CTX - 1)])
    sent(1, b_buf.at[pl.ds(1, CTX - 1)])
    sent(2, c_buf.at[pl.ds(1, CTX - 1)])
    sent(3, d1_buf.at[pl.ds(1, CTX - 1)])
    sent(4, d2_buf.at[pl.ds(1, HEAD - 1)])
    sent(5, d3_buf.at[pl.ds(1, CTX - 1)])
    sent(6, e1_buf.at[pl.ds(1, CTX - 1)])
    sent(7, e2_buf.at[pl.ds(1, HEAD - 1)])


HEAD_SUM = BF16


def body(
    step_inputs, attn_gain, mlp_gain, qkv_trainer, o_trainer, gate_trainer, up_trainer, down_trainer,
    key_page_pool, value_page_pool, page_table, lengths, shard_map,
):
    operands = (
        step_inputs, attn_gain, mlp_gain, qkv_trainer.T, o_trainer, gate_trainer.T, up_trainer.T, down_trainer,
        key_page_pool, value_page_pool, page_table, lengths, shard_map, jnp.asarray(frequency_table()),
    )
    vmem, smem = pltpu.VMEM, pltpu.SMEM
    scratch = [
        vmem((STEPS, RESPONSES, WIDTH), BF16), vmem((WIDTH,), BF16), vmem((WIDTH,), BF16), vmem((8, HEAD_SIZE), F32),
        smem(page_table.shape, jnp.int32), smem((RESPONSES,), jnp.int32), smem((1, CTX), jnp.int32), smem((CTX,), jnp.int32),
        vmem((QKV, D), BF16), vmem((OUT_ROWS, D), BF16), vmem((HIDDEN, D), BF16), vmem((HIDDEN, D), BF16), vmem((HIDDEN, D), BF16),
        vmem(key_page_pool.shape, BF16), vmem(value_page_pool.shape, BF16),
        vmem((CTX, ROWS, MESSAGE), BF16), vmem((ROWS, 128), F32), vmem((CTX, ROWS, 128), F32),
        vmem((ROWS, HEADS, 128), F32), vmem((128, 128), BF16), vmem((128, 128), BF16),
        vmem((HEADS, ROWS, 128), F32), vmem((HEADS, ROWS, 128), F32),
        vmem((CTX, ROWS, 128), F32), vmem((CTX, ROWS, 128), F32),
        vmem((CTX, ROWS, WIDTH), BF16), vmem((CTX, ROWS, WIDTH), BF16), vmem((ROWS, WIDTH), HEAD_SUM), vmem((HEAD, ROWS, WIDTH), HEAD_SUM),
        vmem((CTX, ROWS, MESSAGE), BF16),
        vmem((CTX, ROWS, WIDTH), BF16), vmem((CTX, ROWS, WIDTH), BF16), vmem((ROWS, WIDTH), HEAD_SUM), vmem((HEAD, ROWS, WIDTH), HEAD_SUM),
        vmem((ROWS, WIDTH), F32),
        pltpu.SemaphoreType.DMA((7,)), pltpu.SemaphoreType.DMA((7,)), pltpu.SemaphoreType.DMA((8,)), pltpu.SemaphoreType.DMA((8,)),
        pltpu.SemaphoreType.DMA((CTX,)), pltpu.SemaphoreType.DMA((CTX,)),
    ]
    return pl.pallas_call(
        kernel,
        out_shape=jax.ShapeDtypeStruct((STEPS, RESPONSES, WIDTH), BF16),
        in_specs=[pl.BlockSpec(memory_space=pl.ANY)] * len(operands),
        out_specs=pl.BlockSpec(memory_space=pltpu.VMEM),
        scratch_shapes=scratch,
        compiler_params=pltpu.CompilerParams(
            collective_id=0, has_side_effects=True, vmem_limit_bytes=60 * 1024 * 1024
        ),
    )(*operands)


def solution(mesh):
    in_specs = (
        P(None, None, "ctx"),
        P("ctx"),
        P("ctx"),
        P(None, ("head", "ctx")),
        P(("head", "ctx"), None),
        P(None, ("head", "ctx")),
        P(None, ("head", "ctx")),
        P(("head", "ctx"), None),
        P("ctx", None, "head"),
        P("ctx", None, "head"),
        P(),
        P(),
        P("head", None),
    )
    out_specs = P(None, None, "ctx")
    return jax.shard_map(body, mesh=mesh, in_specs=in_specs, out_specs=out_specs, check_vma=False)
```

```python
import functools

import jax
import jax.numpy as jnp
import numpy as np
from jax import lax
from jax.experimental import pallas as pl
from jax.experimental.pallas import tpu as pltpu
from jax.sharding import PartitionSpec as P

D = 8192
HEAD_SIZE = 128
STEPS = 2
RESPONSES = 8
ROWS = STEPS * RESPONSES
HEADS = 8
CTX = 16
HEAD = 8
WIDTH = D // CTX
TILES = WIDTH // 128
QKV = 80
OUT_ROWS = 64
HIDDEN = 224
PAGES = 16
PAGE = 128
GROUP = 4
MESSAGE = WIDTH + 128
NORM_EPS = 1e-05
ROPE_BASE = 500000.0
NEG = -1e30
F32 = jnp.float32
BF16 = jnp.bfloat16
MESH = pl.DeviceIdType.MESH

HOPS_Y = {0: 0, 1: 1, 2: 2, 3: 1}


def hops(k):
    return HOPS_Y[k // 4] + (k // 2) % 2


NEAR = sorted(range(1, CTX), key=lambda k: (hops(k), k % 2, k))
FAR = NEAR[::-1]


def far_hops(kh, k):
    return HOPS_Y[kh // 2] + HOPS_Y[k // 4] + (0, 1, 2, 1)[kh % 2 + 2 * ((k // 2) % 2)]


def group_of(kh, k):
    return k // 4 * 4 + kh // 2


GROUPS = sorted(range(16), key=lambda g: HOPS_Y[g // 4] + HOPS_Y[g % 4])
EVERYONE = [(kh, k) for kh in range(HEAD) for k in range(CTX) if kh or k]
EVERYONE = sorted(EVERYONE, key=lambda pair: -far_hops(*pair))

NT = (((1,), (1,)), ((), ()))


def frequency_table():
    half = HEAD_SIZE // 2
    f = ROPE_BASE ** (-np.arange(half, dtype=np.float64) * 2.0 / HEAD_SIZE)
    row = np.concatenate([f, f]).astype(np.float32)
    return np.broadcast_to(row[None, :], (8, HEAD_SIZE)).copy()


def tree_sum(terms):
    while len(terms) > 1:
        terms = [functools.reduce(jnp.add, terms[i : i + 2]) for i in range(0, len(terms), 2)]
    return terms[0]


def kernel(
    x_hbm, ag_hbm, mg_hbm, qkv_hbm, o_hbm, gate_hbm, up_hbm, down_hbm, k_hbm, v_hbm,
    pt_hbm, len_hbm, sm_hbm, f_hbm,
    out_ref,
    x_v, ag_v, mg_v, f_v, pt_s, len_s, sm_s, inv_s,
    qkv_w, o_w, gate_w, up_w, down_w, k_w, v_w,
    a_buf, b_send, b_buf, qs, kn, vn, parts, c_send, c_buf,
    d1_send, d1_buf, d3_send, d3_buf, r_send, r_buf, mg_all, e1_send, e1_buf, e2_send, e2_buf,
    small_sem, load_sem, send_sem, recv_sem, a_sem, d3_sem,
):
    h = lax.axis_index("head")
    c = lax.axis_index("ctx")
    h_step = [(1 << i) * (1 - 2 * ((h // (1 << i)) % 2)) for i in range(3)]
    c_step = [(1 << i) * (1 - 2 * ((c // (1 << i)) % 2)) for i in range(4)]

    def ctx_of(k):
        out = c
        for i in range(4):
            if (k >> i) & 1:
                out = out + c_step[i]
        return out

    def head_of(k):
        out = h
        for i in range(3):
            if (k >> i) & 1:
                out = out + h_step[i]
        return out

    def same(k):
        return (h, ctx_of(k))

    def cross(k):
        return (h + h_step[0] if k & 2 else h, ctx_of(k))

    barrier = pltpu.get_barrier_semaphore()
    partners = [cross(k) for k in FAR]
    partners += [(head_of(k), c) for k in range(1, HEAD)]
    for partner in partners:
        pl.semaphore_signal(barrier, inc=1, device_id=partner, device_id_type=MESH)

    small = [(x_hbm, x_v), (ag_hbm, ag_v), (mg_hbm, mg_v), (f_hbm, f_v), (pt_hbm, pt_s), (len_hbm, len_s), (sm_hbm, sm_s)]
    small = [pltpu.make_async_copy(src, dst, small_sem.at[i]) for i, (src, dst) in enumerate(small)]
    for copy in small:
        copy.start()
    large = [(qkv_hbm, qkv_w), (k_hbm, k_w), (v_hbm, v_w), (o_hbm, o_w), (gate_hbm, gate_w), (up_hbm, up_w), (down_hbm, down_w)]
    large = [pltpu.make_async_copy(src, dst, load_sem.at[i]) for i, (src, dst) in enumerate(large)]
    for copy in large:
        copy.start()
    load_qkv, load_k, load_v, load_o, load_gate, load_up, load_down = large
    for copy in small:
        copy.wait()

    row = lax.broadcasted_iota(jnp.int32, (ROWS, 128), 0)
    lane = lax.broadcasted_iota(jnp.int32, (ROWS, 128), 1)

    gains = jnp.concatenate([ag_v[...].astype(F32), mg_v[...].astype(F32)])[None, :]
    tile = jnp.zeros((ROWS, 128), F32)
    for i in range(2 * TILES):
        tile = jnp.where(row == i, gains[:, 128 * i : 128 * (i + 1)], tile)
    a_buf[0, :, :WIDTH] = jnp.concatenate([x_v[0].astype(F32), x_v[1].astype(F32)], axis=0).astype(BF16)
    a_buf[0, :, WIDTH:] = tile.astype(BF16)

    position = jnp.zeros((ROWS, 128), jnp.int32)
    for i in range(ROWS):
        position = jnp.where(row == i, len_s[i % RESPONSES] + i // RESPONSES, position)
    angle = position.astype(F32) * f_v[0:1, :]
    cosine = jnp.cos(angle)
    sine = jnp.sin(angle)
    sine = jnp.where(lane < HEAD_SIZE // 2, -sine, sine)

    for j in range(CTX):
        total = jnp.int32(0)
        for i in range(CTX):
            total = total + jnp.where(sm_s[0, i] == j, jnp.int32(i), jnp.int32(0))
        inv_s[j] = total

    pl.semaphore_wait(barrier, len(partners))

    def exchange(phase, pairs):
        for src, dst, partner in pairs:
            pltpu.make_async_remote_copy(
                src_ref=src, dst_ref=dst, send_sem=send_sem.at[phase], recv_sem=recv_sem.at[phase],
                device_id=partner, device_id_type=MESH,
            ).start()

    def arrived(phase, ref):
        pltpu.make_async_copy(ref, ref, recv_sem.at[phase]).wait()

    def sent(phase, ref):
        pltpu.make_async_copy(ref, ref, send_sem.at[phase]).wait()

    def squares_of(block):
        parts = [block[:, 128 * i : 128 * (i + 1)] for i in range(TILES)]
        return functools.reduce(jnp.add, [p * p for p in parts])

    def row_scale(squares):
        total = jnp.sum(squares, axis=1, keepdims=True)
        return lax.rsqrt(total / D + NORM_EPS)

    for k in FAR:
        pltpu.make_async_remote_copy(
            src_ref=a_buf.at[0], dst_ref=a_buf.at[k], send_sem=send_sem.at[0], recv_sem=a_sem.at[k],
            device_id=cross(k), device_id_type=MESH,
        ).start()

    def gains_of(k):
        rows = a_buf[k, :, WIDTH:].astype(F32)
        mg_all[k] = rows[: 2 * TILES]
        return jnp.concatenate([rows[i : i + 1] for i in range(TILES)], axis=1)

    load_qkv.wait()
    squares = jnp.zeros((ROWS, 128), F32)
    for k in [0] + NEAR:
        if k:
            pltpu.make_async_copy(a_buf.at[k], a_buf.at[k], a_sem.at[k]).wait()
        squares += squares_of(a_buf[k, :, :WIDTH].astype(F32))
    rms = row_scale(squares)
    projected = jnp.zeros((ROWS, QKV), F32)
    for k in range(CTX):
        normed = (a_buf[k, :, :WIDTH].astype(F32) * rms * gains_of(k)).astype(BF16)
        columns = pl.ds(pl.multiple_of(ctx_of(k) * WIDTH, WIDTH), WIDTH)
        projected += lax.dot_general(normed, qkv_w[:, columns], NT, preferred_element_type=F32)

    b_send[...] = jnp.zeros((ROWS, 128), F32)
    b_send[:, :QKV] = projected
    exchange(1, [(b_send, b_buf.at[k], same(k)) for k in FAR])
    b_buf[0] = b_send[...]
    arrived(1, b_buf.at[pl.ds(1, CTX - 1)])

    def slot_of(other):
        slot = jnp.int32(0)
        for i in range(4):
            bit = 1 << i
            slot = slot + bit * ((c // bit + other // bit) % 2)
        return slot

    blocks = [b_buf[slot_of(inv_s[j])] for j in range(CTX)]

    def head_tile(t):
        out = jnp.zeros((ROWS, 128), F32)
        for j in range(CTX):
            start = QKV * j - 128 * t
            if start >= 128 or start + QKV <= 0:
                continue
            piece = blocks[j] if start == 0 else pltpu.roll(blocks[j], start % 128, 1)
            out = jnp.where((lane >= start) & (lane < start + QKV), piece, out)
        return out

    def rope(tile):
        return tile * cosine + pltpu.roll(tile, HEAD_SIZE // 2, 1) * sine

    for t in range(HEADS):
        qs[:, t, :] = rope(head_tile(t))
    kn[...] = jnp.zeros_like(kn)
    vn[...] = jnp.zeros_like(vn)
    kn[:ROWS, :] = rope(head_tile(HEADS)).astype(BF16)
    vn[:ROWS, :] = head_tile(HEADS + 1).astype(BF16)

    load_k.wait()
    load_v.wait()
    scale = HEAD_SIZE ** (-0.5)
    group_row = lax.broadcasted_iota(jnp.int32, (GROUP * ROWS, 128), 0)
    group_lane = lax.broadcasted_iota(jnp.int32, (GROUP * ROWS, 128), 1)
    for first in range(0, RESPONSES, GROUP):
        members = range(first, first + GROUP)
        pages = [[pt_s[r, j * CTX + c] for j in range(PAGES)] for r in members]
        old, new = [], []
        for r, own in zip(members, pages, strict=True):
            q = jnp.concatenate([qs[r], qs[RESPONSES + r]], axis=0).astype(BF16)
            keys = jnp.concatenate([k_w[page] for page in own], axis=0)
            old.append(lax.dot_general(q, keys, NT, preferred_element_type=F32))
            new.append(lax.dot_general(q, kn[...], NT, preferred_element_type=F32))
        length = jnp.concatenate([jnp.full((ROWS, 128), len_s[r], jnp.int32) for r in members], axis=0)
        lives = [(j * CTX + c) * PAGE + group_lane < length for j in range(PAGES)]
        live = (group_lane < ROWS) & (group_lane % RESPONSES == first + group_row // ROWS)
        lives += [live & (group_lane // RESPONSES <= group_row % ROWS // HEADS) & (c == 0)]
        scores = [jnp.concatenate([s[:, PAGE * j : PAGE * (j + 1)] for s in old], axis=0) for j in range(PAGES)]
        scores += [jnp.concatenate(new, axis=0)]
        masked = [jnp.where(live, s * scale, NEG) for s, live in zip(scores, lives, strict=True)]
        top = jnp.max(functools.reduce(jnp.maximum, masked), axis=1, keepdims=True)
        weights = [jnp.where(live, jnp.exp(s - top), 0.0) for s, live in zip(masked, lives, strict=True)]
        total = jnp.sum(functools.reduce(jnp.add, weights), axis=1, keepdims=True)
        both = jnp.where(group_lane < 96, top, total)
        probs = [w.astype(BF16) for w in weights]
        for i, (r, own) in enumerate(zip(members, pages, strict=True)):
            rows = slice(ROWS * i, ROWS * (i + 1))
            values = jnp.concatenate([v_w[page] for page in own], axis=0)
            out = jnp.dot(jnp.concatenate([p[rows] for p in probs[:PAGES]], axis=1), values, preferred_element_type=F32)
            out += jnp.dot(probs[PAGES][rows], vn[...], preferred_element_type=F32)
            for half in range(2):
                shifted = pltpu.roll(out, HEAD_SIZE // 2, 1) if half else out
                message = jnp.where(lane < HEAD_SIZE // 2, shifted, both[rows])
                for s in range(STEPS):
                    parts[half, :, s * RESPONSES + r, :] = message[s * HEADS : (s + 1) * HEADS]

    def half_head(k):
        block = sm_s[0, ctx_of(k)]
        return parts[block % 2, block // 2]

    for k in FAR:
        c_send[k] = half_head(k)
        exchange(2, [(c_send.at[k], c_buf.at[k], same(k))])
    c_buf[0] = half_head(0)
    arrived(2, c_buf.at[pl.ds(1, CTX - 1)])
    received = [c_buf[k] for k in range(CTX)]
    tops = [p[:, 64:65] for p in received]
    top = functools.reduce(jnp.maximum, tops)
    total = jnp.zeros((ROWS, 1), F32)
    out = jnp.zeros((ROWS, 128), F32)
    for p, t in zip(received, tops, strict=True):
        factor = jnp.exp(t - top)
        total = total + factor * p[:, 96:97]
        out = out + factor * p
    attended = (out / total).astype(BF16)[:, :OUT_ROWS]

    def reduce_scatter(phase, left, weight, send, buf):
        for k in FAR + [0]:
            columns = pl.ds(pl.multiple_of(ctx_of(k) * WIDTH, WIDTH), WIDTH)
            block = jnp.dot(left, weight[:, columns], preferred_element_type=F32)
            if k:
                send[k] = block.astype(BF16)
                exchange(phase, [(send.at[k], buf.at[k], cross(k))])
        arrived(phase, buf.at[pl.ds(1, CTX - 1)])
        for k in range(1, CTX):
            block = block + buf[k].astype(F32)
        return block

    def wait_tiles(wait, buf):
        pl.when(reducer)(lambda: wait(buf.at[pl.ds(0, TILES - 1)]))
        pl.when(jnp.logical_not(reducer))(lambda: wait(buf))

    def sum_over_head(phase, block, send, buf):
        send[...] = block.astype(send.dtype)
        exchange(phase, [(send, buf.at[k], (head_of(k), c)) for k in range(HEAD - 1, 0, -1)])
        buf[0] = send[...]
        arrived(phase, buf.at[pl.ds(1, HEAD - 1)])
        total = None
        for other in range(HEAD):
            slot = jnp.int32(0)
            for i in range(3):
                bit = 1 << i
                slot = slot + bit * ((h // bit + other // bit) % 2)
            term = buf[slot].astype(F32)
            total = term if total is None else total + term
        return total

    load_o.wait()
    core = c % 2
    z = h // 2
    reducer = h % 2 == (z + core) % 2
    for k in FAR + [0]:
        other = ctx_of(k)
        columns = pl.ds(pl.multiple_of(other * WIDTH, WIDTH), WIDTH)
        block = jnp.dot(attended, o_w[:, columns], preferred_element_type=F32).astype(BF16)
        for i in range(TILES):
            d1_send[k, i] = block[:, 128 * i : 128 * (i + 1)]
            to = 2 * i + (i + other % 2) % 2
            pair = [(d1_send.at[k, i], d1_buf.at[k * HEAD + h], (to, other))]
            if k:
                exchange(3, pair)
            else:
                pl.when(to != h)(functools.partial(exchange, 3, pair))

    @pl.when(reducer)
    def _():
        d1_buf[h] = d1_send[0, z]
        arrived(3, d1_buf.at[pl.ds(0, CTX * HEAD - 1)])
        totals = [d1_buf[i].astype(F32) for i in range(8)]
        for i in range(8, CTX * HEAD):
            totals[i % 8] = totals[i % 8] + d1_buf[i].astype(F32)
        total = tree_sum(totals)
        columns = pl.ds(pl.multiple_of(z * 128, 128), 128)
        residual = jnp.concatenate([x_v[0, :, columns].astype(F32), x_v[1, :, columns].astype(F32)], axis=0) + total
        r_send[...] = residual
        d3_send[...] = residual.astype(BF16)
        for kh, k in EVERYONE:
            pltpu.make_async_remote_copy(
                src_ref=d3_send, dst_ref=d3_buf.at[group_of(kh, k), k % 4], send_sem=send_sem.at[5], recv_sem=d3_sem.at[group_of(kh, k)],
                device_id=(head_of(kh), ctx_of(k)), device_id_type=MESH,
            ).start()
        d3_buf[0, 0] = residual.astype(BF16)
        exchange(4, [(r_send, r_buf.at[z], (head_of(kh), c)) for kh in range(1, HEAD)])
        r_buf[z] = residual

    def own_group(ref):
        pltpu.make_async_copy(ref, ref, d3_sem.at[0]).wait()

    def z_of(kz):
        out = z
        for i in range(2):
            if (kz >> i) & 1:
                out = out + (1 << i) * (1 - 2 * ((z // (1 << i)) % 2))
        return out

    load_gate.wait()
    load_up.wait()
    gate = jnp.zeros((ROWS, HIDDEN), F32)
    up = jnp.zeros((ROWS, HIDDEN), F32)
    squares = jnp.zeros((ROWS, 128), F32)
    for g in GROUPS:
        if g:
            pltpu.make_async_copy(d3_buf.at[g], d3_buf.at[g], d3_sem.at[g]).wait()
        else:
            pl.when(reducer)(lambda: own_group(d3_buf.at[0, pl.ds(1, TILES - 1)]))
            pl.when(jnp.logical_not(reducer))(lambda: own_group(d3_buf.at[0]))
        tile_z = z_of(g % 4)
        block = jnp.concatenate([d3_buf[g, i].astype(F32) for i in range(TILES)], axis=1)
        gains = [mg_all[g // 4 * 4 + i, pl.ds(TILES + tile_z, 1), :] for i in range(TILES)]
        left = (block * jnp.concatenate(gains, axis=1)).astype(BF16)
        columns = [ctx_of(g // 4 * 4 + i) * WIDTH + tile_z * 128 for i in range(TILES)]
        columns = [pl.ds(pl.multiple_of(column, 128), 128) for column in columns]
        right = jnp.concatenate([gate_w[:, column] for column in columns], axis=1)
        gate += lax.dot_general(left, right, NT, preferred_element_type=F32)
        right = jnp.concatenate([up_w[:, column] for column in columns], axis=1)
        up += lax.dot_general(left, right, NT, preferred_element_type=F32)
        squares += squares_of(block)
    rms = row_scale(squares)
    gate = gate * rms
    up = up * rms
    hidden = (gate / (1.0 + jnp.exp(-gate)) * up).astype(BF16)

    load_down.wait()
    block = reduce_scatter(6, hidden, down_w, e1_send, e1_buf)
    total = sum_over_head(7, block, e2_send, e2_buf)
    wait_tiles(functools.partial(arrived, 4), r_buf)
    decoded = jnp.concatenate([r_buf[i] for i in range(TILES)], axis=1) + total
    out_ref[0] = decoded[:RESPONSES].astype(BF16)
    out_ref[1] = decoded[RESPONSES:].astype(BF16)

    sent(0, a_buf.at[pl.ds(1, CTX - 1)])
    sent(1, b_buf.at[pl.ds(1, CTX - 1)])
    sent(2, c_buf.at[pl.ds(1, CTX - 1)])

    @pl.when(reducer)
    def _():
        sent(3, d1_buf.at[pl.ds(0, CTX * TILES - 1)])
        sent(4, c_buf.at[pl.ds(0, HEAD - 1)])
        sent(5, d1_buf.at[pl.ds(0, CTX * HEAD - 1)])

    @pl.when(jnp.logical_not(reducer))
    def _():
        sent(3, d1_buf.at[pl.ds(0, CTX * TILES)])

    sent(6, e1_buf.at[pl.ds(1, CTX - 1)])
    sent(7, e2_buf.at[pl.ds(1, HEAD - 1)])


HEAD_SUM = BF16


def body(
    step_inputs, attn_gain, mlp_gain, qkv_trainer, o_trainer, gate_trainer, up_trainer, down_trainer,
    key_page_pool, value_page_pool, page_table, lengths, shard_map,
):
    operands = (
        step_inputs, attn_gain, mlp_gain, qkv_trainer.T, o_trainer, gate_trainer.T, up_trainer.T, down_trainer,
        key_page_pool, value_page_pool, page_table, lengths, shard_map, jnp.asarray(frequency_table()),
    )
    vmem, smem = pltpu.VMEM, pltpu.SMEM
    scratch = [
        vmem((STEPS, RESPONSES, WIDTH), BF16), vmem((WIDTH,), BF16), vmem((WIDTH,), BF16), vmem((8, HEAD_SIZE), F32),
        smem(page_table.shape, jnp.int32), smem((RESPONSES,), jnp.int32), smem((1, CTX), jnp.int32), smem((CTX,), jnp.int32),
        vmem((QKV, D), BF16), vmem((OUT_ROWS, D), BF16), vmem((HIDDEN, D), BF16), vmem((HIDDEN, D), BF16), vmem((HIDDEN, D), BF16),
        vmem(key_page_pool.shape, BF16), vmem(value_page_pool.shape, BF16),
        vmem((CTX, ROWS, MESSAGE), BF16), vmem((ROWS, 128), F32), vmem((CTX, ROWS, 128), F32),
        vmem((ROWS, HEADS, 128), F32), vmem((128, 128), BF16), vmem((128, 128), BF16),
        vmem((2, HEADS, ROWS, 128), F32),
        vmem((CTX, ROWS, 128), F32), vmem((CTX, ROWS, 128), F32),
        vmem((CTX, TILES, ROWS, 128), BF16), vmem((CTX * HEAD, ROWS, 128), BF16),
        vmem((ROWS, 128), BF16), vmem((CTX, TILES, ROWS, 128), BF16), vmem((ROWS, 128), F32), vmem((TILES, ROWS, 128), F32), vmem((CTX, 2 * TILES, 128), F32),
        vmem((CTX, ROWS, WIDTH), BF16), vmem((CTX, ROWS, WIDTH), BF16), vmem((ROWS, WIDTH), HEAD_SUM), vmem((HEAD, ROWS, WIDTH), HEAD_SUM),
        pltpu.SemaphoreType.DMA((7,)), pltpu.SemaphoreType.DMA((7,)), pltpu.SemaphoreType.DMA((8,)), pltpu.SemaphoreType.DMA((8,)),
        pltpu.SemaphoreType.DMA((CTX,)), pltpu.SemaphoreType.DMA((CTX,)),
    ]
    return pl.pallas_call(
        kernel,
        out_shape=jax.ShapeDtypeStruct((STEPS, RESPONSES, WIDTH), BF16),
        in_specs=[pl.BlockSpec(memory_space=pl.ANY)] * len(operands),
        out_specs=pl.BlockSpec(memory_space=pltpu.VMEM),
        scratch_shapes=scratch,
        compiler_params=pltpu.CompilerParams(
            collective_id=0, has_side_effects=True, vmem_limit_bytes=60 * 1024 * 1024
        ),
    )(*operands)


def solution(mesh):
    in_specs = (
        P(None, None, "ctx"),
        P("ctx"),
        P("ctx"),
        P(None, ("head", "ctx")),
        P(("head", "ctx"), None),
        P(None, ("head", "ctx")),
        P(None, ("head", "ctx")),
        P(("head", "ctx"), None),
        P("ctx", None, "head"),
        P("ctx", None, "head"),
        P(),
        P(),
        P("head", None),
    )
    out_specs = P(None, None, "ctx")
    return jax.shard_map(body, mesh=mesh, in_specs=in_specs, out_specs=out_specs, check_vma=False)
```

```python
import functools

import jax
import jax.numpy as jnp
import numpy as np
from jax import lax
from jax.experimental import pallas as pl
from jax.experimental.pallas import tpu as pltpu
from jax.sharding import PartitionSpec as P

D = 8192
HEAD_SIZE = 128
STEPS = 2
RESPONSES = 8
ROWS = STEPS * RESPONSES
HEADS = 8
CTX = 16
HEAD = 8
WIDTH = D // CTX
TILES = WIDTH // 128
QKV = 80
OUT_ROWS = 64
HIDDEN = 224
PAGES = 16
PAGE = 128
GROUP = 4
MESSAGE = WIDTH + 128
NORM_EPS = 1e-05
ROPE_BASE = 500000.0
NEG = -1e30
F32 = jnp.float32
BF16 = jnp.bfloat16
MESH = pl.DeviceIdType.MESH

HOPS_Y = {0: 0, 1: 1, 2: 2, 3: 1}


def hops(k):
    return HOPS_Y[k // 4] + (k // 2) % 2


NEAR = sorted(range(1, CTX), key=lambda k: (hops(k), k % 2, k))
FAR = NEAR[::-1]


def far_hops(kh, k):
    return HOPS_Y[kh // 2] + HOPS_Y[k // 4] + (0, 1, 2, 1)[kh % 2 + 2 * ((k // 2) % 2)]


EVERYONE = [(kh, k) for kh in range(HEAD) for k in range(CTX) if kh or k]
EVERYONE = sorted(EVERYONE, key=lambda pair: -far_hops(*pair))

NT = (((1,), (1,)), ((), ()))


def frequency_table():
    half = HEAD_SIZE // 2
    f = ROPE_BASE ** (-np.arange(half, dtype=np.float64) * 2.0 / HEAD_SIZE)
    row = np.concatenate([f, f]).astype(np.float32)
    return np.broadcast_to(row[None, :], (8, HEAD_SIZE)).copy()


def tree_sum(terms):
    while len(terms) > 1:
        terms = [functools.reduce(jnp.add, terms[i : i + 2]) for i in range(0, len(terms), 2)]
    return terms[0]


def kernel(
    x_hbm, ag_hbm, mg_hbm, qkv_hbm, o_hbm, gate_hbm, up_hbm, down_hbm, k_hbm, v_hbm,
    pt_hbm, len_hbm, sm_hbm, f_hbm,
    out_ref,
    x_v, ag_v, mg_v, f_v, pt_s, len_s, sm_s, inv_s,
    qkv_w, o_w, both_w, down_w, k_w, v_w,
    a_buf, b_send, b_buf, qs, kn, vn, parts, c_send, c_buf,
    d1_send, d1_buf, d3_send, d3_buf, r_send, r_buf, mg_all, e1_send, e1_buf, e2_send, e2_buf,
    small_sem, load_sem, send_sem, recv_sem, a_sem, d3_sem,
):
    h = lax.axis_index("head")
    c = lax.axis_index("ctx")
    h_step = [(1 << i) * (1 - 2 * ((h // (1 << i)) % 2)) for i in range(3)]
    c_step = [(1 << i) * (1 - 2 * ((c // (1 << i)) % 2)) for i in range(4)]

    def ctx_of(k):
        out = c
        for i in range(4):
            if (k >> i) & 1:
                out = out + c_step[i]
        return out

    def head_of(k):
        out = h
        for i in range(3):
            if (k >> i) & 1:
                out = out + h_step[i]
        return out

    def same(k):
        return (h, ctx_of(k))

    def cross(k):
        return (h + h_step[0] if k & 2 else h, ctx_of(k))

    small = [(x_hbm, x_v), (ag_hbm, ag_v), (mg_hbm, mg_v), (f_hbm, f_v), (pt_hbm, pt_s), (len_hbm, len_s), (sm_hbm, sm_s)]
    small = [pltpu.make_async_copy(src, dst, small_sem.at[i]) for i, (src, dst) in enumerate(small)]
    for copy in small[:3]:
        copy.start()

    barrier = pltpu.get_barrier_semaphore()
    partners = [cross(k) for k in FAR]
    partners += [(head_of(k), c) for k in range(1, HEAD)]
    for partner in partners:
        pl.semaphore_signal(barrier, inc=1, device_id=partner, device_id_type=MESH)

    for copy in small[3:]:
        copy.start()
    large = [(qkv_hbm, qkv_w), (k_hbm, k_w), (v_hbm, v_w), (o_hbm, o_w), (gate_hbm, both_w.at[pl.ds(0, HIDDEN)]), (up_hbm, both_w.at[pl.ds(HIDDEN, HIDDEN)]), (down_hbm, down_w)]
    large = [pltpu.make_async_copy(src, dst, load_sem.at[i]) for i, (src, dst) in enumerate(large)]
    for copy in large:
        copy.start()
    load_qkv, load_k, load_v, load_o, load_gate, load_up, load_down = large
    for copy in small[:3]:
        copy.wait()

    row = lax.broadcasted_iota(jnp.int32, (ROWS, 128), 0)
    lane = lax.broadcasted_iota(jnp.int32, (ROWS, 128), 1)

    gains = jnp.concatenate([ag_v[...].astype(F32), mg_v[...].astype(F32)])[None, :]
    tile = jnp.zeros((ROWS, 128), F32)
    for i in range(2 * TILES):
        tile = jnp.where(row == i, gains[:, 128 * i : 128 * (i + 1)], tile)
    a_buf[0, :, :WIDTH] = jnp.concatenate([x_v[0].astype(F32), x_v[1].astype(F32)], axis=0).astype(BF16)
    a_buf[0, :, WIDTH:] = tile.astype(BF16)

    pl.semaphore_wait(barrier, len(partners))

    def exchange(phase, pairs):
        for src, dst, partner in pairs:
            pltpu.make_async_remote_copy(
                src_ref=src, dst_ref=dst, send_sem=send_sem.at[phase], recv_sem=recv_sem.at[phase],
                device_id=partner, device_id_type=MESH,
            ).start()

    def arrived(phase, ref):
        pltpu.make_async_copy(ref, ref, recv_sem.at[phase]).wait()

    def sent(phase, ref):
        pltpu.make_async_copy(ref, ref, send_sem.at[phase]).wait()

    def squares_of(block):
        parts = [block[:, 128 * i : 128 * (i + 1)] for i in range(TILES)]
        return functools.reduce(jnp.add, [p * p for p in parts])

    def row_scale(squares):
        total = jnp.sum(squares, axis=1, keepdims=True)
        return lax.rsqrt(total / D + NORM_EPS)

    for k in FAR:
        pltpu.make_async_remote_copy(
            src_ref=a_buf.at[0], dst_ref=a_buf.at[k], send_sem=send_sem.at[0], recv_sem=a_sem.at[k],
            device_id=cross(k), device_id_type=MESH,
        ).start()

    def gains_of(k):
        rows = a_buf[k, :, WIDTH:].astype(F32)
        mg_all[k] = rows[: 2 * TILES]
        return jnp.concatenate([rows[i : i + 1] for i in range(TILES)], axis=1)

    for copy in small[3:]:
        copy.wait()

    position = jnp.zeros((ROWS, 128), jnp.int32)
    for i in range(ROWS):
        position = jnp.where(row == i, len_s[i % RESPONSES] + i // RESPONSES, position)
    angle = position.astype(F32) * f_v[0:1, :]
    cosine = jnp.cos(angle)
    sine = jnp.sin(angle)
    sine = jnp.where(lane < HEAD_SIZE // 2, -sine, sine)

    for j in range(CTX):
        total = jnp.int32(0)
        for i in range(CTX):
            total = total + jnp.where(sm_s[0, i] == j, jnp.int32(i), jnp.int32(0))
        inv_s[j] = total

    kn[...] = jnp.zeros_like(kn)
    vn[...] = jnp.zeros_like(vn)
    load_qkv.wait()
    squares = jnp.zeros((ROWS, 128), F32)
    for k in [0] + NEAR:
        if k:
            pltpu.make_async_copy(a_buf.at[k], a_buf.at[k], a_sem.at[k]).wait()
        squares += squares_of(a_buf[k, :, :WIDTH].astype(F32))
    rms = row_scale(squares)
    projected = jnp.zeros((ROWS, QKV), F32)
    for k in range(CTX):
        normed = (a_buf[k, :, :WIDTH].astype(F32) * rms * gains_of(k)).astype(BF16)
        columns = pl.ds(pl.multiple_of(ctx_of(k) * WIDTH, WIDTH), WIDTH)
        projected += lax.dot_general(normed, qkv_w[:, columns], NT, preferred_element_type=F32)

    b_send[...] = jnp.zeros((ROWS, 128), F32)
    b_send[:, :QKV] = projected
    exchange(1, [(b_send, b_buf.at[k], same(k)) for k in FAR])
    b_buf[0] = b_send[...]
    arrived(1, b_buf.at[pl.ds(1, CTX - 1)])

    def slot_of(other):
        slot = jnp.int32(0)
        for i in range(4):
            bit = 1 << i
            slot = slot + bit * ((c // bit + other // bit) % 2)
        return slot

    blocks = [b_buf[slot_of(inv_s[j])] for j in range(CTX)]

    def head_tile(t):
        out = jnp.zeros((ROWS, 128), F32)
        for j in range(CTX):
            start = QKV * j - 128 * t
            if start >= 128 or start + QKV <= 0:
                continue
            piece = blocks[j] if start == 0 else pltpu.roll(blocks[j], start % 128, 1)
            out = jnp.where((lane >= start) & (lane < start + QKV), piece, out)
        return out

    def rope(tile):
        return tile * cosine + pltpu.roll(tile, HEAD_SIZE // 2, 1) * sine

    for t in range(HEADS):
        qs[:, t, :] = rope(head_tile(t))
    kn[:ROWS, :] = rope(head_tile(HEADS)).astype(BF16)
    vn[:ROWS, :] = head_tile(HEADS + 1).astype(BF16)

    load_k.wait()
    load_v.wait()
    scale = HEAD_SIZE ** (-0.5)
    group_row = lax.broadcasted_iota(jnp.int32, (GROUP * ROWS, 128), 0)
    group_lane = lax.broadcasted_iota(jnp.int32, (GROUP * ROWS, 128), 1)
    for first in range(0, RESPONSES, GROUP):
        members = range(first, first + GROUP)
        pages = [[pt_s[r, j * CTX + c] for j in range(PAGES)] for r in members]
        old, new = [], []
        for r, own in zip(members, pages, strict=True):
            q = jnp.concatenate([qs[r], qs[RESPONSES + r]], axis=0).astype(BF16)
            keys = jnp.concatenate([k_w[page] for page in own], axis=0)
            old.append(lax.dot_general(q, keys, NT, preferred_element_type=F32))
            new.append(lax.dot_general(q, kn[...], NT, preferred_element_type=F32))
        length = jnp.concatenate([jnp.full((ROWS, 128), len_s[r], jnp.int32) for r in members], axis=0)
        lives = [(j * CTX + c) * PAGE + group_lane < length for j in range(PAGES)]
        live = (group_lane < ROWS) & (group_lane % RESPONSES == first + group_row // ROWS)
        lives += [live & (group_lane // RESPONSES <= group_row % ROWS // HEADS) & (c == 0)]
        scores = [jnp.concatenate([s[:, PAGE * j : PAGE * (j + 1)] for s in old], axis=0) for j in range(PAGES)]
        scores += [jnp.concatenate(new, axis=0)]
        masked = [jnp.where(live, s * scale, NEG) for s, live in zip(scores, lives, strict=True)]
        top = jnp.max(functools.reduce(jnp.maximum, masked), axis=1, keepdims=True)
        weights = [jnp.where(live, jnp.exp(s - top), 0.0) for s, live in zip(masked, lives, strict=True)]
        total = jnp.sum(functools.reduce(jnp.add, weights), axis=1, keepdims=True)
        both = jnp.where(group_lane < 96, top, total)
        probs = [w.astype(BF16) for w in weights]
        for i, (r, own) in enumerate(zip(members, pages, strict=True)):
            rows = slice(ROWS * i, ROWS * (i + 1))
            values = jnp.concatenate([v_w[page] for page in own], axis=0)
            out = jnp.dot(jnp.concatenate([p[rows] for p in probs[:PAGES]], axis=1), values, preferred_element_type=F32)
            out += jnp.dot(probs[PAGES][rows], vn[...], preferred_element_type=F32)
            for half in range(2):
                shifted = pltpu.roll(out, HEAD_SIZE // 2, 1) if half else out
                message = jnp.where(lane < HEAD_SIZE // 2, shifted, both[rows])
                for s in range(STEPS):
                    parts[half, :, s * RESPONSES + r, :] = message[s * HEADS : (s + 1) * HEADS]

    def half_head(k):
        block = sm_s[0, ctx_of(k)]
        return parts[block % 2, block // 2]

    for k in FAR:
        c_send[k] = half_head(k)
        exchange(2, [(c_send.at[k], c_buf.at[k], same(k))])
    c_buf[0] = half_head(0)
    arrived(2, c_buf.at[pl.ds(1, CTX - 1)])
    received = [c_buf[k] for k in range(CTX)]
    tops = [p[:, 64:65] for p in received]
    top = functools.reduce(jnp.maximum, tops)
    total = jnp.zeros((ROWS, 1), F32)
    out = jnp.zeros((ROWS, 128), F32)
    for p, t in zip(received, tops, strict=True):
        factor = jnp.exp(t - top)
        total = total + factor * p[:, 96:97]
        out = out + factor * p
    attended = (out / total).astype(BF16)[:, :OUT_ROWS]

    def reduce_scatter(phase, left, weight, send, buf):
        for k in FAR + [0]:
            columns = pl.ds(pl.multiple_of(ctx_of(k) * WIDTH, WIDTH), WIDTH)
            block = jnp.dot(left, weight[:, columns], preferred_element_type=F32)
            if k:
                send[k] = block.astype(BF16)
                exchange(phase, [(send.at[k], buf.at[k], cross(k))])
        arrived(phase, buf.at[pl.ds(1, CTX - 1)])
        for k in range(1, CTX):
            block = block + buf[k].astype(F32)
        return block

    def wait_tiles(wait, buf):
        pl.when(reducer)(lambda: wait(buf.at[pl.ds(0, TILES - 1)]))
        pl.when(jnp.logical_not(reducer))(lambda: wait(buf))

    def sum_over_head(phase, block, send, buf):
        send[...] = block.astype(send.dtype)
        exchange(phase, [(send, buf.at[k], (head_of(k), c)) for k in range(HEAD - 1, 0, -1)])
        buf[0] = send[...]
        arrived(phase, buf.at[pl.ds(1, HEAD - 1)])
        total = None
        for other in range(HEAD):
            slot = jnp.int32(0)
            for i in range(3):
                bit = 1 << i
                slot = slot + bit * ((h // bit + other // bit) % 2)
            term = buf[slot].astype(F32)
            total = term if total is None else total + term
        return total

    load_o.wait()
    core = c % 2
    z = h // 2

    def z_of(kz):
        out = z
        for i in range(2):
            if (kz >> i) & 1:
                out = out + (1 << i) * (1 - 2 * ((z // (1 << i)) % 2))
        return out

    reducer = h % 2 == (z + core) % 2
    for k in FAR + [0]:
        other = ctx_of(k)
        columns = pl.ds(pl.multiple_of(other * WIDTH, WIDTH), WIDTH)
        block = jnp.dot(attended, o_w[:, columns], preferred_element_type=F32).astype(BF16)
        for i in range(TILES):
            d1_send[k, i] = block[:, 128 * i : 128 * (i + 1)]
        for kz in (2, 3, 1, 0):
            i = z_of(kz)
            to = 2 * i + (i + other % 2) % 2
            pair = [(d1_send.at[k, i], d1_buf.at[k * HEAD + h], (to, other))]
            if k or kz:
                exchange(3, pair)
            else:
                pl.when(to != h)(functools.partial(exchange, 3, pair))

    @pl.when(reducer)
    def _():
        d1_buf[h] = d1_send[0, z]
        arrived(3, d1_buf.at[pl.ds(0, CTX * HEAD - 1)])
        totals = [d1_buf[i].astype(F32) for i in range(8)]
        for i in range(8, CTX * HEAD):
            totals[i % 8] = totals[i % 8] + d1_buf[i].astype(F32)
        total = tree_sum(totals)
        columns = pl.ds(pl.multiple_of(z * 128, 128), 128)
        residual = jnp.concatenate([x_v[0, :, columns].astype(F32), x_v[1, :, columns].astype(F32)], axis=0) + total
        r_send[...] = residual
        d3_send[...] = residual.astype(BF16)
        for kh, k in EVERYONE:
            pltpu.make_async_remote_copy(
                src_ref=d3_send, dst_ref=d3_buf.at[k, z], send_sem=send_sem.at[5], recv_sem=d3_sem.at[k],
                device_id=(head_of(kh), ctx_of(k)), device_id_type=MESH,
            ).start()
        d3_buf[0, z] = residual.astype(BF16)
        exchange(4, [(r_send, r_buf.at[z], (head_of(kh), c)) for kh in range(1, HEAD)])
        r_buf[z] = residual

    def own_group(ref):
        pltpu.make_async_copy(ref, ref, d3_sem.at[0]).wait()

    load_gate.wait()
    load_up.wait()
    both = jnp.zeros((ROWS, 2 * HIDDEN), F32)
    squares = jnp.zeros((ROWS, 128), F32)
    for k in [0] + NEAR:
        if k:
            pltpu.make_async_copy(d3_buf.at[k], d3_buf.at[k], d3_sem.at[k]).wait()
        else:
            wait_tiles(own_group, d3_buf.at[0])
        block = jnp.concatenate([d3_buf[k, i].astype(F32) for i in range(TILES)], axis=1)
        gains = jnp.concatenate([mg_all[k, TILES + i : TILES + i + 1, :] for i in range(TILES)], axis=1)
        columns = pl.ds(pl.multiple_of(ctx_of(k) * WIDTH, WIDTH), WIDTH)
        left = (block * gains).astype(BF16)
        both += lax.dot_general(left, both_w[:, columns], NT, preferred_element_type=F32)
        squares += squares_of(block)
    rms = row_scale(squares)
    both = both * rms
    gate, up = both[:, :HIDDEN], both[:, HIDDEN:]
    hidden = (gate / (1.0 + jnp.exp(-gate)) * up).astype(BF16)

    load_down.wait()
    block = reduce_scatter(6, hidden, down_w, e1_send, e1_buf)
    total = sum_over_head(7, block, e2_send, e2_buf)
    wait_tiles(functools.partial(arrived, 4), r_buf)
    decoded = jnp.concatenate([r_buf[i] for i in range(TILES)], axis=1) + total
    out_ref[0] = decoded[:RESPONSES].astype(BF16)
    out_ref[1] = decoded[RESPONSES:].astype(BF16)

    sent(0, a_buf.at[pl.ds(1, CTX - 1)])
    sent(1, b_buf.at[pl.ds(1, CTX - 1)])
    sent(2, c_buf.at[pl.ds(1, CTX - 1)])

    @pl.when(reducer)
    def _():
        sent(3, d1_buf.at[pl.ds(0, CTX * TILES - 1)])
        sent(4, c_buf.at[pl.ds(0, HEAD - 1)])
        sent(5, d1_buf.at[pl.ds(0, CTX * HEAD - 1)])

    @pl.when(jnp.logical_not(reducer))
    def _():
        sent(3, d1_buf.at[pl.ds(0, CTX * TILES)])

    sent(6, e1_buf.at[pl.ds(1, CTX - 1)])
    sent(7, e2_buf.at[pl.ds(1, HEAD - 1)])


HEAD_SUM = BF16


def body(
    step_inputs, attn_gain, mlp_gain, qkv_trainer, o_trainer, gate_trainer, up_trainer, down_trainer,
    key_page_pool, value_page_pool, page_table, lengths, shard_map,
):
    operands = (
        step_inputs, attn_gain, mlp_gain, qkv_trainer.T, o_trainer, gate_trainer.T, up_trainer.T, down_trainer,
        key_page_pool, value_page_pool, page_table, lengths, shard_map, jnp.asarray(frequency_table()),
    )
    vmem, smem = pltpu.VMEM, pltpu.SMEM
    scratch = [
        vmem((STEPS, RESPONSES, WIDTH), BF16), vmem((WIDTH,), BF16), vmem((WIDTH,), BF16), vmem((8, HEAD_SIZE), F32),
        smem(page_table.shape, jnp.int32), smem((RESPONSES,), jnp.int32), smem((1, CTX), jnp.int32), smem((CTX,), jnp.int32),
        vmem((QKV, D), BF16), vmem((OUT_ROWS, D), BF16), vmem((2 * HIDDEN, D), BF16), vmem((HIDDEN, D), BF16),
        vmem(key_page_pool.shape, BF16), vmem(value_page_pool.shape, BF16),
        vmem((CTX, ROWS, MESSAGE), BF16), vmem((ROWS, 128), F32), vmem((CTX, ROWS, 128), F32),
        vmem((ROWS, HEADS, 128), F32), vmem((128, 128), BF16), vmem((128, 128), BF16),
        vmem((2, HEADS, ROWS, 128), F32),
        vmem((CTX, ROWS, 128), F32), vmem((CTX, ROWS, 128), F32),
        vmem((CTX, TILES, ROWS, 128), BF16), vmem((CTX * HEAD, ROWS, 128), BF16),
        vmem((ROWS, 128), BF16), vmem((CTX, TILES, ROWS, 128), BF16), vmem((ROWS, 128), F32), vmem((TILES, ROWS, 128), F32), vmem((CTX, 2 * TILES, 128), F32),
        vmem((CTX, ROWS, WIDTH), BF16), vmem((CTX, ROWS, WIDTH), BF16), vmem((ROWS, WIDTH), HEAD_SUM), vmem((HEAD, ROWS, WIDTH), HEAD_SUM),
        pltpu.SemaphoreType.DMA((7,)), pltpu.SemaphoreType.DMA((7,)), pltpu.SemaphoreType.DMA((8,)), pltpu.SemaphoreType.DMA((8,)),
        pltpu.SemaphoreType.DMA((CTX,)), pltpu.SemaphoreType.DMA((CTX,)),
    ]
    return pl.pallas_call(
        kernel,
        out_shape=jax.ShapeDtypeStruct((STEPS, RESPONSES, WIDTH), BF16),
        in_specs=[pl.BlockSpec(memory_space=pl.ANY)] * len(operands),
        out_specs=pl.BlockSpec(memory_space=pltpu.VMEM),
        scratch_shapes=scratch,
        compiler_params=pltpu.CompilerParams(
            collective_id=0, has_side_effects=True, vmem_limit_bytes=60 * 1024 * 1024
        ),
    )(*operands)


def solution(mesh):
    in_specs = (
        P(None, None, "ctx"),
        P("ctx"),
        P("ctx"),
        P(None, ("head", "ctx")),
        P(("head", "ctx"), None),
        P(None, ("head", "ctx")),
        P(None, ("head", "ctx")),
        P(("head", "ctx"), None),
        P("ctx", None, "head"),
        P("ctx", None, "head"),
        P(),
        P(),
        P("head", None),
    )
    out_specs = P(None, None, "ctx")
    return jax.shard_map(body, mesh=mesh, in_specs=in_specs, out_specs=out_specs, check_vma=False)
```
